32 devices in a mesh: sub: 8 (over z, x), blk: 4 (over y, core).
Axes of the slice: x: 2, y: 2, z: 4, core: 2. Of those that a mesh axis runs over, the one named last changes fastest.
Arguments:
- modes: bfloat16 [16, 2048, 256], P('sub'), may hold values from -0.1875 to 0.1875
- stiff_blocks: bfloat16 [16, 128, 128, 128], P('sub', 'blk'), may hold values from -6 to 6
- mass_blocks: bfloat16 [16, 128, 128, 128], P('sub', 'blk'), may hold values from -6 to 6
- row_index: int32 [16, 128], P('sub', 'blk'), may hold values from 0 to 15
- col_index: int32 [16, 128], P('sub', 'blk'), may hold values from 0 to 3
- live_blocks: int32 [16, 4], P('sub', 'blk'), may hold values from 1 to 32, as said below
- dof_list: int32 [16, 2048], P('sub'), may hold values from 0 to 3071
- parent_basis: bfloat16 [24576, 2048], P('sub', 'blk'), may hold values from -0.125 to 0.125
- level_scale: float32 [8, 2048], P(None, 'blk'), may hold values from 0.35 to 1.4
Outputs:
- ancestor_sum: bfloat16 [8, 2, 256, 2048], P('sub', None, None, 'blk')
The draws below stay inside these ranges and needn't reach their ends.
Inputs may be any that keep to these rules, and one draw needn't show every extreme that they name: live_blocks reaches 32 in every draw.
All inputs are finite; a program needn't handle non-finite values.
Results may differ from the reference program's by a relative error of at most 0.0049.
Values may be sent and summed in bfloat16 or wider, within the bound.
A program may use at most 64 MiB of HBM per device.

```python
import math
import jax
import jax.numpy as jnp
from jax import lax

BLOCK = 128
MODES = 256
NBASIS = 2048
ROWB = 16
COLB_DEV = 4
NNZ_DEV = 32
NP = 3072
LEAF_DEV = 2
MAXLEV = 8
NI = 2048
NF = 2048
LEAVES = 16
SLOTS = 128
PROWS = 24576
N_SUB = 8
N_BLK = 4


def draw_live_blocks(key, part):
    key = jax.random.fold_in(key, 11)
    first, second, third = jax.random.split(key, 3)
    counts = jax.random.randint(first, (LEAVES, N_BLK), 1, NNZ_DEV + 1)
    where_row = jax.random.randint(second, (), 0, LEAVES)
    where_col = jax.random.randint(third, (), 0, N_BLK)
    return counts.at[where_row, where_col].set(NNZ_DEV).astype(jnp.int32)


def set_ends(values, own_key, least, largest):
    place = [jax.random.randint(jax.random.fold_in(own_key, axis), (), 0, length) for axis, length in enumerate(values.shape)]
    main_axis = values.shape.index(max(values.shape))
    neighbour = place[:main_axis] + [(place[main_axis] + 1) % values.shape[main_axis]] + place[main_axis + 1:]
    return values.at[tuple(place)].set(least).at[tuple(neighbour)].set(largest)


def level_of(key, extent, shards, least, high):
    factor_of, own = 1.0, jax.random.fold_in(key, 6)
    for dim, blocks in shards:
        heights = jnp.exp(jax.random.uniform(jax.random.fold_in(own, dim), (blocks,), jnp.float32, least / len(shards), high / len(shards)))
        factor_of = factor_of * jnp.repeat(heights, extent[dim] // blocks).reshape([-1 if axis == dim else 1 for axis in range(len(extent))])
    return factor_of


def bell_draw(own_key, shape, scale, limit, pieces=(), kind=jnp.bfloat16):
    result = jax.random.normal(own_key, shape, jnp.float32) * scale
    if len(pieces) > 0:
        result = level_of(own_key, shape, pieces, -0.22, 0.18) * result
    return jnp.clip(result, min=-limit, max=limit).astype(kind)


def setup_inputs(seed: int = 0) -> dict:
    key_of = jax.random.split(jax.random.key(seed), 10)
    return {
        "modes": bell_draw(key_of[0], (LEAVES, NI, MODES), (BLOCK * NNZ_DEV // COLB_DEV) ** -0.5, 0.1875, ((0, 8),)),
        "stiff_blocks": bell_draw(key_of[1], (LEAVES, SLOTS, BLOCK, BLOCK), 1.0, 6.0, ((0, 8), (1, 4))),
        "mass_blocks": bell_draw(key_of[2], (LEAVES, SLOTS, BLOCK, BLOCK), 0.7, 6.0, ((0, 8), (1, 4))),
        "row_index": set_ends(jax.random.randint(key_of[3], (LEAVES, SLOTS), 0, ROWB), jax.random.fold_in(key_of[3], 1), 0, ROWB - 1).astype(jnp.int32),
        "col_index": set_ends(jax.random.randint(key_of[4], (LEAVES, SLOTS), 0, COLB_DEV), jax.random.fold_in(key_of[4], 1), 0, COLB_DEV - 1).astype(jnp.int32),
        "live_blocks": draw_live_blocks(jax.random.fold_in(key_of[9], 71), 0),
        "dof_list": set_ends(jax.random.randint(key_of[6], (LEAVES, NF), 0, NP), jax.random.fold_in(key_of[6], 1), 0, NP - 1).astype(jnp.int32),
        "parent_basis": bell_draw(key_of[7], (PROWS, NBASIS), NF ** -0.5, 0.125, ((0, 8), (1, 4))),
        "level_scale": jnp.clip(jnp.exp(math.log(1.4) - 1.3862944 * jax.random.uniform(key_of[8], (MAXLEV, NBASIS), jnp.float32) ** level_of(key_of[8], (MAXLEV, NBASIS), ((1, 4),), -0.2, 0.2)), 0.35, 1.4),
    }


def reference(modes, stiff_blocks, mass_blocks, row_index, col_index, live_blocks, dof_list, parent_basis, level_scale):
    bases = parent_basis.reshape(N_SUB, NP, NBASIS)
    slot = jnp.arange(SLOTS, dtype=jnp.int32)
    group = slot // NNZ_DEV

    def one_leaf(leaf):
        phi = modes[leaf].reshape(ROWB, BLOCK, MODES)
        picked = phi[row_index[leaf]].astype(jnp.float32)
        live = (slot % NNZ_DEV) < live_blocks[leaf][group]
        column = group * COLB_DEV + col_index[leaf]
        onehot = ((column[:, None] == jnp.arange(COLB_DEV * N_BLK, dtype=jnp.int32)[None, :]) & live[:, None]).astype(jnp.float32)
        rows = bases[leaf // LEAF_DEV][dof_list[leaf]].astype(jnp.float32)
        outs = []
        for blocks in (stiff_blocks, mass_blocks):
            prod = jnp.einsum('nkr,nkc->nrc', picked, blocks[leaf].astype(jnp.float32), precision=lax.Precision.HIGHEST)
            coupling = jnp.einsum('nrc,ng->rgc', prod, onehot, precision=lax.Precision.HIGHEST).reshape(MODES, NF).astype(jnp.bfloat16)
            outs.append(jnp.dot(coupling.astype(jnp.float32), rows, precision=lax.Precision.HIGHEST))
        return jnp.stack(outs)

    reduced = lax.map(one_leaf, jnp.arange(LEAVES, dtype=jnp.int32))
    reduced = reduced.reshape(N_SUB, LEAF_DEV, 2, MODES, NBASIS)
    node = level_scale[0][None, None, None, :] * (reduced[:, 0] + reduced[:, 1])
    levels = N_SUB.bit_length() - 1
    stored = [node]
    for k in range(1, levels + 1):
        pairs = node.reshape(node.shape[0] // 2, 2, 2, MODES, NBASIS)
        node = level_scale[k][None, None, None, :] * (pairs[:, 0] + pairs[:, 1])
        stored.append(node)
    total = jnp.repeat(stored[levels], N_SUB, axis=0)
    for k in range(levels - 1, -1, -1):
        total = total + jnp.repeat(stored[k], 1 << k, axis=0)
    return total.astype(jnp.bfloat16)
```

```python
import functools

import jax
import jax.numpy as jnp
from jax import lax
from jax.experimental import pallas as pl
from jax.experimental.pallas import tpu as pltpu
from jax.sharding import PartitionSpec as P

COLB_DEV = 4
GROUP = 4
HALVES = 2
MESH = pl.DeviceIdType.MESH


def coupling_kernel(rows_ref, cols_ref, live_ref, modes_ref, stiff_ref, mass_ref, out_ref, phi_t, acc):
    leaf = pl.program_id(0)
    slots, block = stiff_ref.shape[1], stiff_ref.shape[2]
    rowb = modes_ref.shape[1] // block
    half = modes_ref.shape[2] // HALVES
    for r in range(rowb):
        phi_t[r] = modes_ref[0, r * block : (r + 1) * block, :].T
    acc[...] = jnp.zeros_like(acc)
    live = live_ref[leaf, 0]

    def step(g, carry):
        prods = []
        for u in range(GROUP):
            j = g * GROUP + u
            pair = jnp.concatenate([stiff_ref[0, j], mass_ref[0, j]], axis=1)
            prods.append(jnp.dot(phi_t[rows_ref[leaf, j]], pair, preferred_element_type=jnp.float32))
        for u in range(GROUP):
            j = g * GROUP + u
            col = jnp.where(j < live, cols_ref[leaf, j], COLB_DEV)
            acc[col] += prods[u]
        return carry

    lax.fori_loop(0, (live + GROUP - 1) // GROUP, step, 0)
    for c in range(COLB_DEV):
        for m in range(2):
            for h in range(HALVES):
                out_ref[m * HALVES + h, 0, :, c * block : (c + 1) * block] = acc[
                    c, h * half : (h + 1) * half, m * block : (m + 1) * block
                ].astype(out_ref.dtype)


def leaf_couplings(row_index, col_index, live_blocks, modes, stiff, mass):
    leaves, ni, nmodes = modes.shape
    slots, block = stiff.shape[1], stiff.shape[2]
    half = nmodes // HALVES
    return pl.pallas_call(
        coupling_kernel,
        out_shape=jax.ShapeDtypeStruct((2 * HALVES, leaves, half, COLB_DEV * block), jnp.bfloat16),
        grid_spec=pltpu.PrefetchScalarGridSpec(
            num_scalar_prefetch=3,
            grid=(leaves,),
            in_specs=[
                pl.BlockSpec((1, ni, nmodes), lambda l, *_: (l, 0, 0)),
                pl.BlockSpec((1, slots, block, block), lambda l, *_: (l, 0, 0, 0)),
                pl.BlockSpec((1, slots, block, block), lambda l, *_: (l, 0, 0, 0)),
            ],
            out_specs=pl.BlockSpec((2 * HALVES, 1, half, COLB_DEV * block), lambda l, *_: (0, l, 0, 0)),
            scratch_shapes=[
                pltpu.VMEM((ni // block, nmodes, block), jnp.bfloat16),
                pltpu.VMEM((COLB_DEV + 1, nmodes, 2 * block), jnp.float32),
            ],
        ),
        compiler_params=pltpu.CompilerParams(vmem_limit_bytes=40 << 20),
        name="leaf_couplings",
    )(row_index, col_index, live_blocks, modes, stiff, mass)


UNROLL = 32


def rows_kernel(dof_ref, basis_ref, out_ref, table, picked):
    step = pl.program_id(0)
    np_, cols = basis_ref.shape
    nb = cols // 128
    count = out_ref.shape[0]

    @pl.when(step == 0)
    def _():
        for c in range(nb):
            table[pl.ds(c, np_, nb), :] = basis_ref[:, c * 128 : (c + 1) * 128].astype(jnp.float32)

    def body(i, carry):
        for u in range(UNROLL):
            t = i * UNROLL + u
            which = dof_ref[step * count + t]
            picked[pl.ds(t * nb, nb), :] = table[pl.ds(which * nb, nb), :]
        return carry

    lax.fori_loop(0, count // UNROLL, body, 0)
    for c in range(nb):
        out_ref[:, c * 128 : (c + 1) * 128] = picked[pl.ds(c, count, nb), :].astype(out_ref.dtype)


def basis_rows(dof_list, basis):
    total = dof_list.shape[0] * dof_list.shape[1]
    np_, cols = basis.shape
    count = 512
    return pl.pallas_call(
        rows_kernel,
        out_shape=jax.ShapeDtypeStruct((total, cols), jnp.bfloat16),
        grid_spec=pltpu.PrefetchScalarGridSpec(
            num_scalar_prefetch=1,
            grid=(total // count,),
            in_specs=[pl.BlockSpec((np_, cols), lambda i, *_: (0, 0))],
            out_specs=pl.BlockSpec((count, cols), lambda i, *_: (i, 0)),
            scratch_shapes=[
                pltpu.VMEM((np_ * cols // 128, 128), jnp.float32),
                pltpu.VMEM((count * cols // 128, 128), jnp.float32),
            ],
        ),
        compiler_params=pltpu.CompilerParams(vmem_limit_bytes=40 << 20),
        name="basis_rows",
    )(dof_list.reshape(total), basis)


def flipped(index, bit):
    return index + (1 << bit) * (1 - 2 * ((index // (1 << bit)) % 2))


def merge_kernel(
    levels, c_ref, rows_hbm, scale_ref, out_ref,
    rows, got, node0, part, node, total, sends, merged, t_send, t_got,
    rows_sem, y_send, y_recv, core_send, core_recv, fwd_send, fwd_recv, lev_send, lev_recv, t_ssem, t_rsem,
):
    q, b = lax.axis_index("sub"), lax.axis_index("blk")
    chunks, leaves, depth, width = c_ref.shape
    rows_copy = pltpu.make_async_copy(rows_hbm, rows, rows_sem)
    rows_copy.start()
    near, far = (q, flipped(b, 0)), (q, flipped(b, 1))
    peers = [(flipped(q, k), b) for k in range(levels)]
    barrier = pltpu.get_barrier_semaphore()
    for peer in [near, far] + peers:
        pl.semaphore_signal(barrier, inc=1, device_id=peer, device_id_type=MESH)
    pl.semaphore_wait(barrier, 2 + levels)

    def remote(src, dst, ssem, rsem, peer):
        return pltpu.make_async_remote_copy(
            src_ref=src, dst_ref=dst, send_sem=ssem, recv_sem=rsem, device_id=peer, device_id_type=MESH
        )

    far_copies = [remote(c_ref.at[i], got.at[1, i], y_send.at[i], y_recv.at[i], far) for i in range(chunks)]
    near_copies = [remote(c_ref.at[i], got.at[0, i], core_send.at[i], core_recv.at[i], near) for i in range(chunks)]
    fwd_copies = [remote(got.at[1, i], got.at[2, i], fwd_send.at[i], fwd_recv.at[i], near) for i in range(chunks)]
    lev_copies = [
        [remote(sends.at[k, i], merged.at[k, i], lev_send.at[k, i], lev_recv.at[k, i], peers[k]) for i in range(chunks)]
        for k in range(levels)
    ]
    t_copies = [remote(t_send.at[i], t_got.at[i], t_ssem.at[i], t_rsem.at[i], peers[0]) for i in range(chunks)]
    for copy in far_copies + near_copies:
        copy.start()
    rows_copy.wait()

    def product(tile, which):
        res = None
        for leaf in range(leaves):
            start = pl.multiple_of((leaf * 4 + which) * width, width)
            one = jnp.dot(tile[leaf], rows[pl.ds(start, width), :], preferred_element_type=jnp.float32)
            res = one if res is None else res + one
        return res

    half = depth // 2
    own = q % 2
    for i in range(chunks):
        part[i] = product(c_ref.at[i], b)
    for i in range(chunks):
        near_copies[i].wait_recv()
        part[i] += product(got.at[0, i], near[1])

    def leaf_stage(i):
        far_copies[i].wait_recv()
        fwd_copies[i].start()
        part[i] += product(got.at[1, i], far[1])
        fwd_copies[i].wait_recv()
        res = scale_ref[0:1, :] * (part[i] + product(got.at[2, i], flipped(far[1], 0)))
        node0[i, 0] = res[:half]
        node0[i, 1] = res[half:]
        if levels:
            sends[0, i] = node0[i, 1 - own].astype(sends.dtype)
            lev_copies[0][i].start()

    def level_stage(k, i):
        lev_copies[k - 1][i].wait_recv()
        mine = node0[i, own] if k == 1 else node[i]
        value = scale_ref[k : k + 1, :] * (mine + merged[k - 1, i].astype(jnp.float32))
        node[i] = value
        summed = value if k == 1 else total[i] + value
        total[i] = summed
        if k < levels:
            sends[k, i] = value.astype(sends.dtype)
            lev_copies[k][i].start()
        else:
            t_send[i] = summed.astype(t_send.dtype)
            t_copies[i].start()
            out_ref[i, own] = (node0[i, own] + summed).astype(out_ref.dtype)

    def last_stage(i):
        t_copies[i].wait_recv()
        out_ref[i, 1 - own] = (node0[i, 1 - own] + t_got[i].astype(jnp.float32)).astype(out_ref.dtype)

    stages = [leaf_stage] + [functools.partial(level_stage, k) for k in range(1, levels + 1)] + [last_stage]
    for t in range(chunks + len(stages) - 1):
        for s, stage in enumerate(stages):
            if 0 <= t - s < chunks:
                stage(t - s)
    for copy in far_copies + near_copies + fwd_copies + [c for row in lev_copies for c in row] + t_copies:
        copy.wait_send()


def merged_tree(coupling, rows, level_scale, levels):
    chunks, leaves, depth, width = coupling.shape
    cols = rows.shape[1]
    half = depth // 2
    bf, f32 = jnp.bfloat16, jnp.float32
    dma = pltpu.SemaphoreType.DMA
    vmem = pl.BlockSpec(memory_space=pltpu.VMEM)
    return pl.pallas_call(
        functools.partial(merge_kernel, levels),
        out_shape=jax.ShapeDtypeStruct((chunks, 2, half, cols), bf),
        in_specs=[vmem, pl.BlockSpec(memory_space=pl.ANY), vmem],
        out_specs=vmem,
        scratch_shapes=[
            pltpu.VMEM(rows.shape, bf),
            pltpu.VMEM((3, chunks, leaves, depth, width), bf),
            pltpu.VMEM((chunks, 2, half, cols), f32),
            pltpu.VMEM((chunks, depth, cols), f32),
            pltpu.VMEM((chunks, half, cols), f32),
            pltpu.VMEM((chunks, half, cols), f32),
            pltpu.VMEM((levels, chunks, half, cols), bf),
            pltpu.VMEM((levels, chunks, half, cols), bf),
            pltpu.VMEM((chunks, half, cols), bf),
            pltpu.VMEM((chunks, half, cols), bf),
            dma,
            dma((chunks,)), dma((chunks,)), dma((chunks,)), dma((chunks,)), dma((chunks,)), dma((chunks,)),
            dma((levels, chunks)), dma((levels, chunks)), dma((chunks,)), dma((chunks,)),
        ],
        compiler_params=pltpu.CompilerParams(
            collective_id=0, has_side_effects=True, vmem_limit_bytes=40 << 20
        ),
        name="merged_tree",
    )(coupling, rows, level_scale)


def per_device(
    modes,
    stiff_blocks,
    mass_blocks,
    row_index,
    col_index,
    live_blocks,
    dof_list,
    parent_basis,
    level_scale,
):
    levels = lax.axis_size("sub").bit_length() - 1
    coupling = leaf_couplings(row_index, col_index, live_blocks, modes, stiff_blocks, mass_blocks)
    rows = basis_rows(dof_list, parent_basis)
    out = merged_tree(coupling, rows, level_scale, levels)
    return out.reshape(1, 2, modes.shape[2], parent_basis.shape[1])


def solution(mesh):
    in_specs = (
        P("sub", None, None),
        P("sub", "blk", None, None),
        P("sub", "blk", None, None),
        P("sub", "blk"),
        P("sub", "blk"),
        P("sub", "blk"),
        P("sub", None),
        P("sub", "blk"),
        P(None, "blk"),
    )
    out_specs = P("sub", None, None, "blk")
    return jax.shard_map(
        per_device, mesh=mesh, in_specs=in_specs, out_specs=out_specs, check_vma=False
    )
```

```python
import functools

import jax
import jax.numpy as jnp
from jax import lax
from jax.experimental import pallas as pl
from jax.experimental.pallas import tpu as pltpu
from jax.sharding import PartitionSpec as P

COLB_DEV = 4
GROUP = 4
HALVES = 4
MESH = pl.DeviceIdType.MESH


def coupling_kernel(
    rows_hbm, cols_hbm, live_hbm, modes_ref, stiff_ref, mass_ref, out_ref,
    phi_t, acc, rows_ref, cols_ref, live_ref, sems,
):
    leaf = pl.program_id(0)
    fetches = [
        pltpu.make_async_copy(src, dst, sems.at[n])
        for n, (src, dst) in enumerate(((rows_hbm, rows_ref), (cols_hbm, cols_ref), (live_hbm, live_ref)))
    ]

    @pl.when(leaf == 0)
    def _():
        for fetch in fetches:
            fetch.start()

    slots, block = stiff_ref.shape[1], stiff_ref.shape[2]
    rowb = modes_ref.shape[1] // block
    half = modes_ref.shape[2] // HALVES
    for r in range(rowb):
        phi_t[r] = modes_ref[0, r * block : (r + 1) * block, :].T
    acc[...] = jnp.zeros_like(acc)

    @pl.when(leaf == 0)
    def _():
        for fetch in fetches:
            fetch.wait()

    live = live_ref[leaf, 0]

    def step(g, carry):
        prods = []
        for u in range(GROUP):
            j = g * GROUP + u
            pair = jnp.concatenate([stiff_ref[0, j], mass_ref[0, j]], axis=1)
            prods.append(jnp.dot(phi_t[rows_ref[leaf, j]], pair, preferred_element_type=jnp.float32))
        for u in range(GROUP):
            j = g * GROUP + u
            col = jnp.where(j < live, cols_ref[leaf, j], COLB_DEV)
            acc[col] += prods[u]
        return carry

    lax.fori_loop(0, (live + GROUP - 1) // GROUP, step, 0)
    for c in range(COLB_DEV):
        for m in range(2):
            for h in range(HALVES):
                out_ref[m * HALVES + h, 0, :, c * block : (c + 1) * block] = acc[
                    c, h * half : (h + 1) * half, m * block : (m + 1) * block
                ].astype(out_ref.dtype)


def leaf_couplings(row_index, col_index, live_blocks, modes, stiff, mass):
    leaves, ni, nmodes = modes.shape
    slots, block = stiff.shape[1], stiff.shape[2]
    half = nmodes // HALVES
    return pl.pallas_call(
        coupling_kernel,
        out_shape=jax.ShapeDtypeStruct((2 * HALVES, leaves, half, COLB_DEV * block), jnp.bfloat16),
        grid_spec=pl.GridSpec(
            grid=(leaves,),
            in_specs=[pl.BlockSpec(memory_space=pl.ANY)] * 3 + [
                pl.BlockSpec((1, ni, nmodes), lambda l: (l, 0, 0)),
                pl.BlockSpec((1, slots, block, block), lambda l: (l, 0, 0, 0)),
                pl.BlockSpec((1, slots, block, block), lambda l: (l, 0, 0, 0)),
            ],
            out_specs=pl.BlockSpec((2 * HALVES, 1, half, COLB_DEV * block), lambda l: (0, l, 0, 0)),
            scratch_shapes=[
                pltpu.VMEM((ni // block, nmodes, block), jnp.bfloat16),
                pltpu.VMEM((COLB_DEV + 1, nmodes, 2 * block), jnp.float32),
                pltpu.SMEM(row_index.shape, jnp.int32),
                pltpu.SMEM(col_index.shape, jnp.int32),
                pltpu.SMEM(live_blocks.shape, jnp.int32),
                pltpu.SemaphoreType.DMA((3,)),
            ],
        ),
        compiler_params=pltpu.CompilerParams(vmem_limit_bytes=62 << 20),
        name="leaf_couplings",
    )(row_index, col_index, live_blocks, modes, stiff, mass)


UNROLL = 32


def flipped(index, bit):
    return index + (1 << bit) * (1 - 2 * ((index // (1 << bit)) % 2))


def merge_kernel(
    levels, c_ref, dof_hbm, basis_hbm, scale_ref, out_ref,
    dof_ref, basis, table, picked, rows, got, node0, part, node, total, sends, merged, t_send, t_got,
    dof_sem, basis_sem, y_send, y_recv, core_send, core_recv, fwd_send, fwd_recv, lev_send, lev_recv, t_ssem, t_rsem,
):
    q, b = lax.axis_index("sub"), lax.axis_index("blk")
    chunks, leaves, depth, width = c_ref.shape
    dof_copy = pltpu.make_async_copy(dof_hbm, dof_ref, dof_sem)
    basis_copy = pltpu.make_async_copy(basis_hbm, basis, basis_sem)
    dof_copy.start()
    basis_copy.start()
    near, far = (q, flipped(b, 0)), (q, flipped(b, 1))
    peers = [(flipped(q, k), b) for k in range(levels)]
    barrier = pltpu.get_barrier_semaphore()
    for peer in [near, far] + peers:
        pl.semaphore_signal(barrier, inc=1, device_id=peer, device_id_type=MESH)
    pl.semaphore_wait(barrier, 2 + levels)

    def remote(src, dst, ssem, rsem, peer):
        return pltpu.make_async_remote_copy(
            src_ref=src, dst_ref=dst, send_sem=ssem, recv_sem=rsem, device_id=peer, device_id_type=MESH
        )

    far_copies = [remote(c_ref.at[i], got.at[1, i], y_send.at[i], y_recv.at[i], far) for i in range(chunks)]
    near_copies = [remote(c_ref.at[i], got.at[0, i], core_send.at[i], core_recv.at[i], near) for i in range(chunks)]
    fwd_copies = [remote(got.at[1, i], got.at[2, i], fwd_send.at[i], fwd_recv.at[i], near) for i in range(chunks)]
    lev_copies = [
        [remote(sends.at[k, i], merged.at[k, i], lev_send.at[k, i], lev_recv.at[k, i], peers[k]) for i in range(chunks)]
        for k in range(levels)
    ]
    t_copies = [remote(t_send.at[i], t_got.at[i], t_ssem.at[i], t_rsem.at[i], peers[0]) for i in range(chunks)]
    for copy in far_copies + near_copies:
        copy.start()
    dof_copy.wait()
    basis_copy.wait()
    np_, cols = basis.shape
    nb = cols // 128
    count = dof_ref.shape[1]
    for c in range(nb):
        table[pl.ds(c, np_, nb), :] = basis[:, c * 128 : (c + 1) * 128].astype(jnp.float32)
    for leaf in range(leaves):

        def pick(i, carry, leaf=leaf):
            for u in range(UNROLL):
                which = dof_ref[leaf, i * UNROLL + u]
                picked[pl.ds((i * UNROLL + u) * nb, nb), :] = table[pl.ds(which * nb, nb), :]
            return carry

        lax.fori_loop(0, count // UNROLL, pick, 0)
        for c in range(nb):
            rows[pl.ds(leaf * count, count), c * 128 : (c + 1) * 128] = picked[pl.ds(c, count, nb), :].astype(rows.dtype)

    def product(tile, which):
        res = None
        for leaf in range(leaves):
            start = pl.multiple_of((leaf * 4 + which) * width, width)
            one = jnp.dot(tile[leaf], rows[pl.ds(start, width), :], preferred_element_type=jnp.float32)
            res = one if res is None else res + one
        return res

    half = depth // 2
    own = q % 2
    for i in range(chunks):
        near_copies[i].wait_recv()
    batch = chunks // 2
    for g in range(2):
        res = None
        for leaf in range(leaves):
            for ref, which in ((c_ref, b), (got.at[0], near[1])):
                tile = ref[pl.ds(g * batch, batch), leaf].reshape(batch * depth, width)
                start = pl.multiple_of((leaf * 4 + which) * width, width)
                one = jnp.dot(tile, rows[pl.ds(start, width), :], preferred_element_type=jnp.float32)
                res = one if res is None else res + one
        part[pl.ds(g * batch, batch)] = res.reshape(batch, depth, cols)

    def leaf_stage(i):
        far_copies[i].wait_recv()
        fwd_copies[i].start()
        part[i] += product(got.at[1, i], far[1])
        fwd_copies[i].wait_recv()
        res = scale_ref[0:1, :] * (part[i] + product(got.at[2, i], flipped(far[1], 0)))
        node0[i, 0] = res[:half]
        node0[i, 1] = res[half:]
        if levels:
            sends[0, i] = node0[i, 1 - own].astype(sends.dtype)
            lev_copies[0][i].start()

    def level_stage(k, i):
        lev_copies[k - 1][i].wait_recv()
        mine = node0[i, own] if k == 1 else node[i]
        value = scale_ref[k : k + 1, :] * (mine + merged[k - 1, i].astype(jnp.float32))
        node[i] = value
        summed = value if k == 1 else total[i] + value
        total[i] = summed
        if k < levels:
            sends[k, i] = value.astype(sends.dtype)
            lev_copies[k][i].start()
        else:
            t_send[i] = summed.astype(t_send.dtype)
            t_copies[i].start()
            out_ref[i, own] = (node0[i, own] + summed).astype(out_ref.dtype)

    def last_stage(i):
        t_copies[i].wait_recv()
        out_ref[i, 1 - own] = (node0[i, 1 - own] + t_got[i].astype(jnp.float32)).astype(out_ref.dtype)

    stages = [leaf_stage] + [functools.partial(level_stage, k) for k in range(1, levels + 1)] + [last_stage]
    for t in range(chunks + len(stages) - 1):
        for s, stage in enumerate(stages):
            if 0 <= t - s < chunks:
                stage(t - s)
    for copy in far_copies + near_copies + fwd_copies + [c for row in lev_copies for c in row] + t_copies:
        copy.wait_send()


def merged_tree(coupling, dof_list, basis, level_scale, levels):
    chunks, leaves, depth, width = coupling.shape
    np_, cols = basis.shape
    nf = dof_list.shape[1]
    half = depth // 2
    bf, f32 = jnp.bfloat16, jnp.float32
    dma = pltpu.SemaphoreType.DMA
    vmem = pl.BlockSpec(memory_space=pltpu.VMEM)
    return pl.pallas_call(
        functools.partial(merge_kernel, levels),
        out_shape=jax.ShapeDtypeStruct((chunks, 2, half, cols), bf),
        in_specs=[vmem] + [pl.BlockSpec(memory_space=pl.ANY)] * 2 + [vmem],
        out_specs=vmem,
        scratch_shapes=[
            pltpu.SMEM(dof_list.shape, jnp.int32),
            pltpu.VMEM(basis.shape, bf),
            pltpu.VMEM((np_ * cols // 128, 128), f32),
            pltpu.VMEM((nf * cols // 128, 128), f32),
            pltpu.VMEM((leaves * nf, cols), bf),
            pltpu.VMEM((3, chunks, leaves, depth, width), bf),
            pltpu.VMEM((chunks, 2, half, cols), f32),
            pltpu.VMEM((chunks, depth, cols), f32),
            pltpu.VMEM((chunks, half, cols), f32),
            pltpu.VMEM((chunks, half, cols), f32),
            pltpu.VMEM((levels, chunks, half, cols), bf),
            pltpu.VMEM((levels, chunks, half, cols), bf),
            pltpu.VMEM((chunks, half, cols), bf),
            pltpu.VMEM((chunks, half, cols), bf),
            dma, dma,
            dma((chunks,)), dma((chunks,)), dma((chunks,)), dma((chunks,)), dma((chunks,)), dma((chunks,)),
            dma((levels, chunks)), dma((levels, chunks)), dma((chunks,)), dma((chunks,)),
        ],
        compiler_params=pltpu.CompilerParams(
            collective_id=0, has_side_effects=True, vmem_limit_bytes=40 << 20
        ),
        name="merged_tree",
    )(coupling, dof_list, basis, level_scale)


def per_device(
    modes,
    stiff_blocks,
    mass_blocks,
    row_index,
    col_index,
    live_blocks,
    dof_list,
    parent_basis,
    level_scale,
):
    levels = lax.axis_size("sub").bit_length() - 1
    coupling = leaf_couplings(row_index, col_index, live_blocks, modes, stiff_blocks, mass_blocks)
    out = merged_tree(coupling, dof_list, parent_basis, level_scale, levels)
    return out.reshape(1, 2, modes.shape[2], parent_basis.shape[1])


def solution(mesh):
    in_specs = (
        P("sub", None, None),
        P("sub", "blk", None, None),
        P("sub", "blk", None, None),
        P("sub", "blk"),
        P("sub", "blk"),
        P("sub", "blk"),
        P("sub", None),
        P("sub", "blk"),
        P(None, "blk"),
    )
    out_specs = P("sub", None, None, "blk")
    return jax.shard_map(
        per_device, mesh=mesh, in_specs=in_specs, out_specs=out_specs, check_vma=False
    )
```

```python
import functools

import jax
import jax.numpy as jnp
from jax import lax
from jax.experimental import pallas as pl
from jax.experimental.pallas import tpu as pltpu
from jax.sharding import PartitionSpec as P

COLB_DEV = 4
GROUP = 4
HALVES = 2
MESH = pl.DeviceIdType.MESH


def coupling_kernel(
    rows_hbm, cols_hbm, live_hbm, modes_ref, stiff_ref, mass_ref, out_ref,
    phi_t, acc, rows_ref, cols_ref, live_ref, sems,
):
    leaf = pl.program_id(0)
    fetches = [
        pltpu.make_async_copy(src, dst, sems.at[n])
        for n, (src, dst) in enumerate(((rows_hbm, rows_ref), (cols_hbm, cols_ref), (live_hbm, live_ref)))
    ]

    @pl.when(leaf == 0)
    def _():
        for fetch in fetches:
            fetch.start()

    slots, block = stiff_ref.shape[1], stiff_ref.shape[2]
    rowb = modes_ref.shape[1] // block
    half = modes_ref.shape[2] // HALVES
    for r in range(rowb):
        phi_t[r] = modes_ref[0, r * block : (r + 1) * block, :].T
    acc[...] = jnp.zeros_like(acc)

    @pl.when(leaf == 0)
    def _():
        for fetch in fetches:
            fetch.wait()

    live = live_ref[0, leaf]

    def step(g, carry):
        prods = []
        for u in range(GROUP):
            j = g * GROUP + u
            pair = jnp.concatenate([stiff_ref[0, j], mass_ref[0, j]], axis=1)
            prods.append(jnp.dot(phi_t[rows_ref[leaf, j]], pair, preferred_element_type=jnp.float32))
        for u in range(GROUP):
            j = g * GROUP + u
            col = jnp.where(j < live, cols_ref[leaf, j], COLB_DEV)
            acc[col] += prods[u]
        return carry

    lax.fori_loop(0, (live + GROUP - 1) // GROUP, step, 0)
    for c in range(COLB_DEV):
        for m in range(2):
            for h in range(HALVES):
                out_ref[m * HALVES + h, 0, :, c * block : (c + 1) * block] = acc[
                    c, h * half : (h + 1) * half, m * block : (m + 1) * block
                ].astype(out_ref.dtype)


def leaf_couplings(row_index, col_index, live_blocks, modes, stiff, mass):
    leaves, ni, nmodes = modes.shape
    slots, block = stiff.shape[1], stiff.shape[2]
    half = nmodes // HALVES
    return pl.pallas_call(
        coupling_kernel,
        out_shape=jax.ShapeDtypeStruct((2 * HALVES, leaves, half, COLB_DEV * block), jnp.bfloat16),
        grid_spec=pl.GridSpec(
            grid=(leaves,),
            in_specs=[pl.BlockSpec(memory_space=pl.ANY)] * 3 + [
                pl.BlockSpec((1, ni, nmodes), lambda l: (l, 0, 0)),
                pl.BlockSpec((1, slots, block, block), lambda l: (l, 0, 0, 0)),
                pl.BlockSpec((1, slots, block, block), lambda l: (l, 0, 0, 0)),
            ],
            out_specs=pl.BlockSpec((2 * HALVES, 1, half, COLB_DEV * block), lambda l: (0, l, 0, 0)),
            scratch_shapes=[
                pltpu.VMEM((ni // block, nmodes, block), jnp.bfloat16),
                pltpu.VMEM((COLB_DEV + 1, nmodes, 2 * block), jnp.float32),
                pltpu.SMEM(row_index.shape, jnp.int32),
                pltpu.SMEM(col_index.shape, jnp.int32),
                pltpu.SMEM(live_blocks.shape, jnp.int32),
                pltpu.SemaphoreType.DMA((3,)),
            ],
        ),
        compiler_params=pltpu.CompilerParams(vmem_limit_bytes=62 << 20),
        name="leaf_couplings",
    )(row_index, col_index, live_blocks, modes, stiff, mass)


UNROLL = 32


def flipped(index, bit):
    return index + (1 << bit) * (1 - 2 * ((index // (1 << bit)) % 2))


def merge_kernel(
    levels, c_hbm, dof_hbm, basis_hbm, scale_ref, out_ref,
    c_ref, dof_ref, basis, table, picked, rows, got, node0, part, node, total, sends, merged, t_send, t_got,
    c_sem, dof_sem, basis_sem, y_send, y_recv, core_send, core_recv, fwd_send, fwd_recv, lev_send, lev_recv, t_ssem, t_rsem,
):
    q, b = lax.axis_index("sub"), lax.axis_index("blk")
    chunks, leaves, depth, width = c_hbm.shape
    c_copy = pltpu.make_async_copy(c_hbm, c_ref, c_sem)
    dof_copy = pltpu.make_async_copy(dof_hbm, dof_ref, dof_sem)
    basis_copy = pltpu.make_async_copy(basis_hbm, basis, basis_sem)
    dof_copy.start()
    c_copy.start()
    basis_copy.start()
    near, far = (q, flipped(b, 0)), (q, flipped(b, 1))
    peers = [(flipped(q, k), b) for k in range(levels)]
    barrier = pltpu.get_barrier_semaphore()
    for peer in [near, far] + peers:
        pl.semaphore_signal(barrier, inc=1, device_id=peer, device_id_type=MESH)
    pl.semaphore_wait(barrier, 2 + levels)

    def remote(src, dst, ssem, rsem, peer):
        return pltpu.make_async_remote_copy(
            src_ref=src, dst_ref=dst, send_sem=ssem, recv_sem=rsem, device_id=peer, device_id_type=MESH
        )

    far_copies = [remote(c_hbm.at[i], got.at[1, i], y_send.at[i], y_recv.at[i], far) for i in range(chunks)]
    near_copies = [remote(c_hbm.at[i], got.at[0, i], core_send.at[i], core_recv.at[i], near) for i in range(chunks)]
    fwd_copies = [remote(got.at[1, i], got.at[2, i], fwd_send.at[i], fwd_recv.at[i], near) for i in range(chunks)]
    lev_copies = [
        [remote(sends.at[k, i], merged.at[k, i], lev_send.at[k, i], lev_recv.at[k, i], peers[k]) for i in range(chunks)]
        for k in range(levels)
    ]
    t_copies = [remote(t_send.at[i], t_got.at[i], t_ssem.at[i], t_rsem.at[i], peers[0]) for i in range(chunks)]
    for copy in far_copies + near_copies:
        copy.start()
    dof_copy.wait()
    c_copy.wait()
    basis_copy.wait()
    np_, cols = basis.shape
    nb = cols // 128
    count = dof_ref.shape[1]
    for c in range(nb):
        table[pl.ds(c, np_, nb), :] = basis[:, c * 128 : (c + 1) * 128].astype(jnp.float32)
    for leaf in range(leaves):

        def pick(i, carry, leaf=leaf):
            for u in range(UNROLL):
                which = dof_ref[leaf, i * UNROLL + u]
                picked[pl.ds((i * UNROLL + u) * nb, nb), :] = table[pl.ds(which * nb, nb), :]
            return carry

        lax.fori_loop(0, count // UNROLL, pick, 0)
        for c in range(nb):
            rows[pl.ds(leaf * count, count), c * 128 : (c + 1) * 128] = picked[pl.ds(c, count, nb), :].astype(rows.dtype)

    def product(tile, which):
        res = None
        for leaf in range(leaves):
            start = pl.multiple_of((leaf * 4 + which) * width, width)
            one = jnp.dot(tile[leaf], rows[pl.ds(start, width), :], preferred_element_type=jnp.float32)
            res = one if res is None else res + one
        return res

    half = depth // 2
    own = q % 2
    for i in range(chunks):
        near_copies[i].wait_recv()
    batch = chunks // 2
    for g in range(2):
        res = None
        for leaf in range(leaves):
            for ref, which in ((c_ref, b), (got.at[0], near[1])):
                tile = ref[pl.ds(g * batch, batch), leaf].reshape(batch * depth, width)
                start = pl.multiple_of((leaf * 4 + which) * width, width)
                one = jnp.dot(tile, rows[pl.ds(start, width), :], preferred_element_type=jnp.float32)
                res = one if res is None else res + one
        part[pl.ds(g * batch, batch)] = res.reshape(batch, depth, cols)

    def leaf_stage(i):
        far_copies[i].wait_recv()
        fwd_copies[i].start()
        part[i] += product(got.at[1, i], far[1])
        fwd_copies[i].wait_recv()
        res = scale_ref[0:1, :] * (part[i] + product(got.at[2, i], flipped(far[1], 0)))
        node0[i, 0] = res[:half]
        node0[i, 1] = res[half:]
        if levels:
            sends[0, i] = node0[i, 1 - own].astype(sends.dtype)
            lev_copies[0][i].start()

    def level_stage(k, i):
        lev_copies[k - 1][i].wait_recv()
        mine = node0[i, own] if k == 1 else node[i]
        value = scale_ref[k : k + 1, :] * (mine + merged[k - 1, i].astype(jnp.float32))
        node[i] = value
        summed = value if k == 1 else total[i] + value
        total[i] = summed
        if k < levels:
            sends[k, i] = value.astype(sends.dtype)
            lev_copies[k][i].start()
        else:
            t_send[i] = summed.astype(t_send.dtype)
            t_copies[i].start()
            out_ref[i, own] = (node0[i, own] + summed).astype(out_ref.dtype)

    def last_stage(i):
        t_copies[i].wait_recv()
        out_ref[i, 1 - own] = (node0[i, 1 - own] + t_got[i].astype(jnp.float32)).astype(out_ref.dtype)

    stages = [leaf_stage] + [functools.partial(level_stage, k) for k in range(1, levels + 1)] + [last_stage]
    for t in range(2 * (chunks - 1) + len(stages)):
        for s, stage in enumerate(stages):
            if (t - s) % 2 == 0 and 0 <= t - s < 2 * chunks:
                stage((t - s) // 2)
    for copy in far_copies + near_copies + fwd_copies + [c for row in lev_copies for c in row] + t_copies:
        copy.wait_send()


def merged_tree(coupling, dof_list, basis, level_scale, levels):
    chunks, leaves, depth, width = coupling.shape
    np_, cols = basis.shape
    nf = dof_list.shape[1]
    half = depth // 2
    bf, f32 = jnp.bfloat16, jnp.float32
    dma = pltpu.SemaphoreType.DMA
    vmem = pl.BlockSpec(memory_space=pltpu.VMEM)
    return pl.pallas_call(
        functools.partial(merge_kernel, levels),
        out_shape=jax.ShapeDtypeStruct((chunks, 2, half, cols), bf),
        in_specs=[pl.BlockSpec(memory_space=pl.ANY)] * 3 + [vmem],
        out_specs=vmem,
        scratch_shapes=[
            pltpu.VMEM(coupling.shape, bf),
            pltpu.SMEM(dof_list.shape, jnp.int32),
            pltpu.VMEM(basis.shape, bf),
            pltpu.VMEM((np_ * cols // 128, 128), f32),
            pltpu.VMEM((nf * cols // 128, 128), f32),
            pltpu.VMEM((leaves * nf, cols), bf),
            pltpu.VMEM((3, chunks, leaves, depth, width), bf),
            pltpu.VMEM((chunks, 2, half, cols), f32),
            pltpu.VMEM((chunks, depth, cols), f32),
            pltpu.VMEM((chunks, half, cols), f32),
            pltpu.VMEM((chunks, half, cols), f32),
            pltpu.VMEM((levels, chunks, half, cols), bf),
            pltpu.VMEM((levels, chunks, half, cols), bf),
            pltpu.VMEM((chunks, half, cols), bf),
            pltpu.VMEM((chunks, half, cols), bf),
            dma, dma, dma,
            dma((chunks,)), dma((chunks,)), dma((chunks,)), dma((chunks,)), dma((chunks,)), dma((chunks,)),
            dma((levels, chunks)), dma((levels, chunks)), dma((chunks,)), dma((chunks,)),
        ],
        compiler_params=pltpu.CompilerParams(
            collective_id=0, has_side_effects=True, vmem_limit_bytes=62 << 20
        ),
        name="merged_tree",
    )(coupling, dof_list, basis, level_scale)


def per_device(
    modes,
    stiff_blocks,
    mass_blocks,
    row_index,
    col_index,
    live_blocks,
    dof_list,
    parent_basis,
    level_scale,
):
    levels = lax.axis_size("sub").bit_length() - 1
    coupling = leaf_couplings(row_index, col_index, live_blocks.T, modes, stiff_blocks, mass_blocks)
    out = merged_tree(coupling, dof_list, parent_basis, level_scale, levels)
    return out.reshape(1, 2, modes.shape[2], parent_basis.shape[1])


def solution(mesh):
    in_specs = (
        P("sub", None, None),
        P("sub", "blk", None, None),
        P("sub", "blk", None, None),
        P("sub", "blk"),
        P("sub", "blk"),
        P("sub", "blk"),
        P("sub", None),
        P("sub", "blk"),
        P(None, "blk"),
    )
    out_specs = P("sub", None, None, "blk")
    return jax.shard_map(
        per_device, mesh=mesh, in_specs=in_specs, out_specs=out_specs, check_vma=False
    )
```

```python
import functools

import jax
import jax.numpy as jnp
from jax import lax
from jax.experimental import pallas as pl
from jax.experimental.pallas import tpu as pltpu
from jax.sharding import PartitionSpec as P

COLB_DEV = 4
GROUP = 4
HALVES = 2
MESH = pl.DeviceIdType.MESH


def coupling_kernel(
    rows_hbm, cols_hbm, live_hbm, modes_ref, stiff_ref, mass_ref, out_ref,
    phi_t, acc, rows_ref, cols_ref, live_ref, sems,
):
    leaf = pl.program_id(0)
    fetches = [
        pltpu.make_async_copy(src, dst, sems.at[n])
        for n, (src, dst) in enumerate(((rows_hbm, rows_ref), (cols_hbm, cols_ref), (live_hbm, live_ref)))
    ]

    @pl.when(leaf == 0)
    def _():
        for fetch in fetches:
            fetch.start()

    slots, block = stiff_ref.shape[1], stiff_ref.shape[2]
    rowb = modes_ref.shape[1] // block
    half = modes_ref.shape[2] // HALVES
    for r in range(rowb):
        phi_t[r] = modes_ref[0, r * block : (r + 1) * block, :].T
    acc[...] = jnp.zeros_like(acc)

    @pl.when(leaf == 0)
    def _():
        for fetch in fetches:
            fetch.wait()

    live = live_ref[0, leaf]

    def step(g, carry):
        prods = []
        for u in range(GROUP):
            j = g * GROUP + u
            pair = jnp.concatenate([stiff_ref[0, j], mass_ref[0, j]], axis=1)
            prods.append(jnp.dot(phi_t[rows_ref[leaf, j]], pair, preferred_element_type=jnp.float32))
        for u in range(GROUP):
            j = g * GROUP + u
            col = jnp.where(j < live, cols_ref[leaf, j], COLB_DEV)
            acc[col] += prods[u]
        return carry

    lax.fori_loop(0, (live + GROUP - 1) // GROUP, step, 0)
    for c in range(COLB_DEV):
        for m in range(2):
            for h in range(HALVES):
                out_ref[m * HALVES + h, 0, :, c * block : (c + 1) * block] = acc[
                    c, h * half : (h + 1) * half, m * block : (m + 1) * block
                ].astype(out_ref.dtype)


def leaf_couplings(row_index, col_index, live_blocks, modes, stiff, mass):
    leaves, ni, nmodes = modes.shape
    slots, block = stiff.shape[1], stiff.shape[2]
    half = nmodes // HALVES
    return pl.pallas_call(
        coupling_kernel,
        out_shape=jax.ShapeDtypeStruct((2 * HALVES, leaves, half, COLB_DEV * block), jnp.bfloat16),
        grid_spec=pl.GridSpec(
            grid=(leaves,),
            in_specs=[pl.BlockSpec(memory_space=pl.ANY)] * 3 + [
                pl.BlockSpec((1, ni, nmodes), lambda l: (l, 0, 0)),
                pl.BlockSpec((1, slots, block, block), lambda l: (l, 0, 0, 0)),
                pl.BlockSpec((1, slots, block, block), lambda l: (l, 0, 0, 0)),
            ],
            out_specs=pl.BlockSpec((2 * HALVES, 1, half, COLB_DEV * block), lambda l: (0, l, 0, 0)),
            scratch_shapes=[
                pltpu.VMEM((ni // block, nmodes, block), jnp.bfloat16),
                pltpu.VMEM((COLB_DEV + 1, nmodes, 2 * block), jnp.float32),
                pltpu.SMEM(row_index.shape, jnp.int32),
                pltpu.SMEM(col_index.shape, jnp.int32),
                pltpu.SMEM(live_blocks.shape, jnp.int32),
                pltpu.SemaphoreType.DMA((3,)),
            ],
        ),
        compiler_params=pltpu.CompilerParams(vmem_limit_bytes=62 << 20),
        name="leaf_couplings",
    )(row_index, col_index, live_blocks, modes, stiff, mass)


UNROLL = 32


def flipped(index, bit):
    return index + (1 << bit) * (1 - 2 * ((index // (1 << bit)) % 2))


def merge_kernel(
    levels, c_hbm, dof_hbm, basis_hbm, scale_ref, out_ref,
    c_ref, dof_ref, basis, table, picked, rows, got, node0, part, node, total, sends, merged, t_send, t_got,
    c_sem, dof_sem, basis_sem, y_send, y_recv, core_send, core_recv, fwd_send, fwd_recv, lev_send, lev_recv, t_ssem, t_rsem,
):
    q, b = lax.axis_index("sub"), lax.axis_index("blk")
    chunks, leaves, depth, width = c_hbm.shape
    c_copy = pltpu.make_async_copy(c_hbm, c_ref, c_sem)
    dof_copy = pltpu.make_async_copy(dof_hbm, dof_ref, dof_sem)
    basis_copy = pltpu.make_async_copy(basis_hbm, basis, basis_sem)
    dof_copy.start()
    c_copy.start()
    basis_copy.start()
    near, far = (q, flipped(b, 0)), (q, flipped(b, 1))
    peers = [(flipped(q, k), b) for k in range(levels)]
    barrier = pltpu.get_barrier_semaphore()
    for peer in [near, far] + peers:
        pl.semaphore_signal(barrier, inc=1, device_id=peer, device_id_type=MESH)
    pl.semaphore_wait(barrier, 2 + levels)

    def remote(src, dst, ssem, rsem, peer):
        return pltpu.make_async_remote_copy(
            src_ref=src, dst_ref=dst, send_sem=ssem, recv_sem=rsem, device_id=peer, device_id_type=MESH
        )

    far_copies = [remote(c_hbm.at[i], got.at[1, i], y_send.at[i], y_recv.at[i], far) for i in range(chunks)]
    near_copies = [remote(c_hbm.at[i], got.at[0, i], core_send.at[i], core_recv.at[i], near) for i in range(chunks)]
    fwd_copies = [remote(got.at[1, i], got.at[2, i], fwd_send.at[i], fwd_recv.at[i], near) for i in range(chunks)]
    lev_copies = [
        [remote(sends.at[k, i], merged.at[k, i], lev_send.at[k, i], lev_recv.at[k, i], peers[k]) for i in range(chunks)]
        for k in range(levels)
    ]
    t_copies = [remote(t_send.at[i], t_got.at[i], t_ssem.at[i], t_rsem.at[i], peers[0]) for i in range(chunks)]
    early = chunks // 2
    for copy in far_copies[:early] + near_copies:
        copy.start()
    dof_copy.wait()
    c_copy.wait()
    basis_copy.wait()
    np_, cols = basis.shape
    nb = cols // 128
    count = dof_ref.shape[1]
    for c in range(nb):
        table[pl.ds(c, np_, nb), :] = basis[:, c * 128 : (c + 1) * 128].astype(jnp.float32)
    for leaf in range(leaves):

        def pick(i, carry, leaf=leaf):
            for u in range(UNROLL):
                which = dof_ref[leaf, i * UNROLL + u]
                picked[pl.ds((i * UNROLL + u) * nb, nb), :] = table[pl.ds(which * nb, nb), :]
            return carry

        lax.fori_loop(0, count // UNROLL, pick, 0)
        for c in range(nb):
            rows[pl.ds(leaf * count, count), c * 128 : (c + 1) * 128] = picked[pl.ds(c, count, nb), :].astype(rows.dtype)

    def product(tile, which):
        res = None
        for leaf in range(leaves):
            start = pl.multiple_of((leaf * 4 + which) * width, width)
            one = jnp.dot(tile[leaf], rows[pl.ds(start, width), :], preferred_element_type=jnp.float32)
            res = one if res is None else res + one
        return res

    for copy in far_copies[:early]:
        copy.wait_send()
    for copy in far_copies[early:]:
        copy.start()
    half = depth // 2
    own = q % 2
    for i in range(chunks):
        near_copies[i].wait_recv()
    batch = chunks // 2
    for g in range(2):
        res = None
        for leaf in range(leaves):
            for ref, which in ((c_ref, b), (got.at[0], near[1])):
                tile = ref[pl.ds(g * batch, batch), leaf].reshape(batch * depth, width)
                start = pl.multiple_of((leaf * 4 + which) * width, width)
                one = jnp.dot(tile, rows[pl.ds(start, width), :], preferred_element_type=jnp.float32)
                res = one if res is None else res + one
        part[pl.ds(g * batch, batch)] = res.reshape(batch, depth, cols)

    def leaf_stage(i):
        far_copies[i].wait_recv()
        fwd_copies[i].start()
        part[i] += product(got.at[1, i], far[1])
        fwd_copies[i].wait_recv()
        res = scale_ref[0:1, :] * (part[i] + product(got.at[2, i], flipped(far[1], 0)))
        node0[i, 0] = res[:half]
        node0[i, 1] = res[half:]
        if levels:
            sends[0, i] = node0[i, 1 - own].astype(sends.dtype)
            lev_copies[0][i].start()

    def level_stage(k, i):
        lev_copies[k - 1][i].wait_recv()
        mine = node0[i, own] if k == 1 else node[i]
        value = scale_ref[k : k + 1, :] * (mine + merged[k - 1, i].astype(jnp.float32))
        node[i] = value
        summed = value if k == 1 else total[i] + value
        total[i] = summed
        if k < levels:
            sends[k, i] = value.astype(sends.dtype)
            lev_copies[k][i].start()
        else:
            t_send[i] = summed.astype(t_send.dtype)
            t_copies[i].start()
            out_ref[i, own] = (node0[i, own] + summed).astype(out_ref.dtype)

    def last_stage(i):
        t_copies[i].wait_recv()
        out_ref[i, 1 - own] = (node0[i, 1 - own] + t_got[i].astype(jnp.float32)).astype(out_ref.dtype)

    stages = [leaf_stage] + [functools.partial(level_stage, k) for k in range(1, levels + 1)] + [last_stage]
    for t in range(2 * (chunks - 1) + len(stages)):
        for s, stage in enumerate(stages):
            if (t - s) % 2 == 0 and 0 <= t - s < 2 * chunks:
                stage((t - s) // 2)
    for copy in far_copies[early:] + near_copies + fwd_copies + [c for row in lev_copies for c in row] + t_copies:
        copy.wait_send()


def merged_tree(coupling, dof_list, basis, level_scale, levels):
    chunks, leaves, depth, width = coupling.shape
    np_, cols = basis.shape
    nf = dof_list.shape[1]
    half = depth // 2
    bf, f32 = jnp.bfloat16, jnp.float32
    dma = pltpu.SemaphoreType.DMA
    vmem = pl.BlockSpec(memory_space=pltpu.VMEM)
    return pl.pallas_call(
        functools.partial(merge_kernel, levels),
        out_shape=jax.ShapeDtypeStruct((chunks, 2, half, cols), bf),
        in_specs=[pl.BlockSpec(memory_space=pl.ANY)] * 3 + [vmem],
        out_specs=vmem,
        scratch_shapes=[
            pltpu.VMEM(coupling.shape, bf),
            pltpu.SMEM(dof_list.shape, jnp.int32),
            pltpu.VMEM(basis.shape, bf),
            pltpu.VMEM((np_ * cols // 128, 128), f32),
            pltpu.VMEM((nf * cols // 128, 128), f32),
            pltpu.VMEM((leaves * nf, cols), bf),
            pltpu.VMEM((3, chunks, leaves, depth, width), bf),
            pltpu.VMEM((chunks, 2, half, cols), f32),
            pltpu.VMEM((chunks, depth, cols), f32),
            pltpu.VMEM((chunks, half, cols), f32),
            pltpu.VMEM((chunks, half, cols), f32),
            pltpu.VMEM((levels, chunks, half, cols), bf),
            pltpu.VMEM((levels, chunks, half, cols), bf),
            pltpu.VMEM((chunks, half, cols), bf),
            pltpu.VMEM((chunks, half, cols), bf),
            dma, dma, dma,
            dma((chunks,)), dma((chunks,)), dma((chunks,)), dma((chunks,)), dma((chunks,)), dma((chunks,)),
            dma((levels, chunks)), dma((levels, chunks)), dma((chunks,)), dma((chunks,)),
        ],
        compiler_params=pltpu.CompilerParams(
            collective_id=0, has_side_effects=True, vmem_limit_bytes=62 << 20
        ),
        name="merged_tree",
    )(coupling, dof_list, basis, level_scale)


def per_device(
    modes,
    stiff_blocks,
    mass_blocks,
    row_index,
    col_index,
    live_blocks,
    dof_list,
    parent_basis,
    level_scale,
):
    levels = lax.axis_size("sub").bit_length() - 1
    coupling = leaf_couplings(row_index, col_index, live_blocks.T, modes, stiff_blocks, mass_blocks)
    out = merged_tree(coupling, dof_list, parent_basis, level_scale, levels)
    return out.reshape(1, 2, modes.shape[2], parent_basis.shape[1])


def solution(mesh):
    in_specs = (
        P("sub", None, None),
        P("sub", "blk", None, None),
        P("sub", "blk", None, None),
        P("sub", "blk"),
        P("sub", "blk"),
        P("sub", "blk"),
        P("sub", None),
        P("sub", "blk"),
        P(None, "blk"),
    )
    out_specs = P("sub", None, None, "blk")
    return jax.shard_map(
        per_device, mesh=mesh, in_specs=in_specs, out_specs=out_specs, check_vma=False
    )
```
